256 devices in a mesh: lib: 32 (over y, z), mp: 8 (over x, core).
Axes of the slice: x: 4, y: 4, z: 8, core: 2. Of those that a mesh axis runs over, the one named last changes fastest.
Arguments:
- output_basis: bfloat16 [12288, 512], P('mp'), may hold values from -6 to 6
- input_basis: bfloat16 [12288, 512], P('mp'), may hold values from -6 to 6
- adapter_up_factor: bfloat16 [1024, 16, 12288], P('lib', None, 'mp'), may hold values from -6 to 6
- adapter_down_factor: bfloat16 [1024, 16, 12288], P('lib', None, 'mp'), may hold values from -6 to 6
- slot_adapter_index: int32 [1024], P('lib'), may hold values from 0 to 1023, each once
- shard_live_counts: int32 [32], replicated, may hold values from 1 to 32, 256 in all
- adapter_usage_weight: float32 [1024], replicated, may hold values from 1 to 10
Outputs:
- basis_out_next: bfloat16 [12288, 512], P('mp')
- basis_in_next: bfloat16 [12288, 512], P('mp')
The draws below stay inside these ranges and needn't reach their ends.
Inputs may be any that keep to these rules, and one draw needn't show every extreme that they name: `slot_adapter_index`: every adapter of the library appears in exactly one slot. `shard_live_counts`: the counts sum to 256; some shard holds exactly 32 live slots.
All inputs are finite; a program needn't handle non-finite values.
Results may differ from the reference program's by a relative error of at most 0.017.
Values may be sent and summed in bfloat16 or wider, within the bound.
No kernel may reach another device: no remote copies, remote signals or barrier semaphores. Data moves between devices by JAX's collectives and lax.ppermute only.
A program may use at most 128 MiB of HBM per device.

```python
import math
import jax
import jax.numpy as jnp
import numpy as np
from jax import lax

MODEL_WIDTH = 12288
K = 512
ADAPTER_RANK = 16
SWEEPS = 1
SHARD_CAPACITY = 32
TOTAL = 256
N_LIB = 32


def common_part(key, count, lowest, highest):
    total = jnp.zeros((MODEL_WIDTH, K), jnp.float32)
    for number in range(count):
        sub_key = jax.random.fold_in(key, 100 + number)
        sign_key, column_key = jax.random.split(sub_key)
        amplitude = lowest * (highest / lowest) ** (number / (count - 1))
        row_signs = jax.random.rademacher(sign_key, (MODEL_WIDTH, 1), dtype=jnp.float32)
        column_load = jax.random.normal(column_key, (1, K), dtype=jnp.float32)
        total = total + amplitude * row_signs * column_load
    return total


def draw_output_basis(key, part):
    key = jax.random.fold_in(key, 11)
    noise_key, shape_key = jax.random.split(key)
    noise_field = jax.random.normal(noise_key, (MODEL_WIDTH, K), jnp.float32)
    common = common_part(shape_key, 8, 0.3, 1.5)
    return jnp.clip(noise_field + common, -6.0, 6.0).astype(jnp.bfloat16)


def draw_input_basis(key, part):
    key = jax.random.fold_in(key, 12)
    noise_key, shape_key = jax.random.split(key)
    noise_field = jax.random.normal(noise_key, (MODEL_WIDTH, K), jnp.float32)
    common = common_part(shape_key, 8, 0.3, 1.5)
    return jnp.clip(noise_field + common, -6.0, 6.0).astype(jnp.bfloat16)


def block_scale(key, extent, shards, least, high):
    def one(position, parts):
        steps = jax.random.uniform(jax.random.fold_in(jax.random.fold_in(key, 6), position), (parts,), jnp.float32, least / len(shards), high / len(shards))
        return jnp.repeat(jnp.exp(steps), extent[position] // parts).reshape((-1,) + (1,) * (len(extent) - position - 1))

    level = one(*shards[0])
    for cut in shards[1:]:
        level = level * one(*cut)
    return level


def profile(amount, total, reach, lean):
    loads = [(1 << 20) // math.isqrt(rank ** lean) + 1 for rank in range(2, amount + 1)]
    rest, given = total - reach - (amount - 1), [1] * (amount - 1)
    while rest > 0:
        movable = [i for i in range(amount - 1) if given[i] < reach]
        pool, left = sum([loads[i] for i in movable]), rest
        for i in movable:
            more = min(reach - given[i], max(1, left * loads[i] // pool), rest)
            given[i] = given[i] + more
            rest = rest - more
    return np.array([reach] + given)


def ragged_sizes(stream_key, number_of, total, bound, lean):
    if number_of == 2:
        one = jax.random.randint(stream_key, (), max(1, total - bound), min(bound, total - 1) + 1)
        return jnp.stack([one, total - one])
    sizes = jnp.asarray(profile(number_of, total, bound, lean), jnp.int32)
    twos = (number_of - 1) // 2
    giver, sink = sizes[1:1 + 2 * twos:2], sizes[2:2 + 2 * twos:2]
    slack = jnp.minimum(giver - 1, bound - sink)
    passed = jax.random.randint(jax.random.fold_in(stream_key, 1), (twos,), 0, 1 << 20) % (slack + 1)
    sizes = sizes.at[1:1 + 2 * twos:2].set(giver - passed).at[2:2 + 2 * twos:2].set(sink + passed)
    return sizes[jax.random.permutation(jax.random.fold_in(stream_key, 2), number_of)]


def normal_values(stream_key, shape, width, reach, shards=(), kind=jnp.bfloat16):
    drawn = jax.random.normal(stream_key, shape, jnp.float32) * width
    if len(shards) > 0:
        drawn = block_scale(stream_key, shape, shards, -0.22, 0.18) * drawn
    return jnp.clip(drawn, min=-reach, max=reach).astype(kind)


def setup_inputs(seed: int = 0) -> dict:
    keys = jax.random.split(jax.random.key(seed), 8)
    output_basis = draw_output_basis(jax.random.fold_in(keys[7], 71), 0)
    input_basis = draw_input_basis(jax.random.fold_in(keys[7], 71), 0)
    adapter_up_factor = normal_values(keys[2], (N_LIB * SHARD_CAPACITY, ADAPTER_RANK, MODEL_WIDTH), 1.0, 6.0, ((0, 32), (2, 8)))
    adapter_down_factor = normal_values(keys[3], (N_LIB * SHARD_CAPACITY, ADAPTER_RANK, MODEL_WIDTH), 1.0, 6.0, ((0, 32), (2, 8)))
    slot_adapter_index = jax.random.permutation(keys[4], N_LIB * SHARD_CAPACITY).astype(jnp.int32)
    shard_live_counts = ragged_sizes(keys[5], N_LIB, TOTAL, SHARD_CAPACITY, 2).astype(jnp.int32)
    adapter_usage_weight = jnp.clip(jnp.exp(jax.random.uniform(keys[6], (N_LIB * SHARD_CAPACITY,), jnp.float32, math.log(1.0), math.log(10.0))), 1.0, 10.0)
    return {"output_basis": output_basis, "input_basis": input_basis, "adapter_up_factor": adapter_up_factor, "adapter_down_factor": adapter_down_factor, "slot_adapter_index": slot_adapter_index, "shard_live_counts": shard_live_counts, "adapter_usage_weight": adapter_usage_weight}


PRECISE = lax.Precision.HIGHEST
CORE_RIDGE = 0.25
BASIS_PENALTY = 0.1

def blocked_cholesky(matrix):
    matrix_size = matrix.shape[0]
    block_step = min(128, matrix_size)
    lower_factor = jnp.zeros_like(matrix)
    for block_start in range(0, matrix_size, block_step):
        block_stop = block_start + block_step
        finished = lower_factor[:, :block_start]
        column_panel = matrix[block_start:, block_start:block_stop] - jnp.dot(finished[block_start:], finished[block_start:block_stop].T, precision=PRECISE)
        diagonal_block = jnp.linalg.cholesky(column_panel[:block_step])
        if block_stop < matrix_size:
            below_block = jax.scipy.linalg.solve_triangular(diagonal_block, column_panel[block_step:].T, lower=True).T
            new_columns = jnp.concatenate([diagonal_block, below_block], axis=0)
        else:
            new_columns = diagonal_block
        lower_factor = lower_factor.at[block_start:, block_start:block_stop].set(new_columns)
    return lower_factor

def solve_from_right(row_block, factor):
    return jax.scipy.linalg.cho_solve((factor, True), row_block.T).T

def adapter_summands(projected_up, projected_down, fitting_weight, output_factor, input_factor, core_penalty_shift, adapter_rank_size):
    basis_width = projected_up.shape[1]
    total_slot_count = projected_up.shape[0] // adapter_rank_size
    output_fitting = solve_from_right(projected_up, output_factor).reshape(total_slot_count, adapter_rank_size, basis_width)
    input_fitting = solve_from_right(projected_down, input_factor).reshape(total_slot_count, adapter_rank_size, basis_width)
    up_row_list = projected_up.reshape(total_slot_count, adapter_rank_size, basis_width)
    down_row_list = projected_down.reshape(total_slot_count, adapter_rank_size, basis_width)
    cross_out = jnp.einsum('crk,csk->crs', down_row_list, input_fitting, precision=PRECISE)
    cross_in = jnp.einsum('crk,csk->crs', up_row_list, output_fitting, precision=PRECISE)
    curve_out = cross_out - core_penalty_shift * jnp.einsum('crk,csk->crs', input_fitting, input_fitting, precision=PRECISE)
    curve_in = cross_in - core_penalty_shift * jnp.einsum('crk,csk->crs', output_fitting, output_fitting, precision=PRECISE)
    scaled = fitting_weight[:, None, None]
    output_contribution = scaled * jnp.einsum('crs,csk->crk', cross_out, output_fitting, precision=PRECISE)
    input_contribution = scaled * jnp.einsum('crs,csk->crk', cross_in, input_fitting, precision=PRECISE)
    load_out = scaled * jnp.einsum('crs,csk->crk', curve_out, output_fitting, precision=PRECISE)
    load_in = scaled * jnp.einsum('crs,csk->crk', curve_in, input_fitting, precision=PRECISE)
    normal_out = jnp.einsum('crk,crl->kl', load_out, output_fitting, precision=PRECISE)
    normal_in = jnp.einsum('crk,crl->kl', load_in, input_fitting, precision=PRECISE)
    output_contribution = output_contribution.reshape(-1, basis_width).astype(jnp.bfloat16)
    input_contribution = input_contribution.reshape(-1, basis_width).astype(jnp.bfloat16)
    return (output_contribution, input_contribution, normal_out, normal_in)

def reference(output_basis, input_basis, adapter_up_factor, adapter_down_factor, slot_adapter_index, shard_live_counts, adapter_usage_weight):
    slot_index = jnp.arange(N_LIB * SHARD_CAPACITY, dtype=jnp.int32)
    live_limit = jnp.repeat(shard_live_counts, SHARD_CAPACITY)
    fitting_weight = jnp.where(slot_index % SHARD_CAPACITY < live_limit, adapter_usage_weight[slot_adapter_index], 0.0).astype(jnp.float32)
    every_adapter = jnp.sum(shard_live_counts).astype(jnp.float32)
    identity_k = jnp.eye(K, dtype=jnp.float32)
    core_penalty_shift = CORE_RIDGE * MODEL_WIDTH
    basis_penalty_shift = BASIS_PENALTY * ADAPTER_RANK * K * every_adapter / MODEL_WIDTH
    flattened_up = adapter_up_factor.reshape(-1, MODEL_WIDTH)
    flattened_down = adapter_down_factor.reshape(-1, MODEL_WIDTH)
    for sweep_no in range(SWEEPS):
        gram_out = jnp.dot(output_basis.T.astype(jnp.float32), output_basis.astype(jnp.float32), preferred_element_type=jnp.float32)
        gram_in = jnp.dot(input_basis.T.astype(jnp.float32), input_basis.astype(jnp.float32), preferred_element_type=jnp.float32)
        projected_up = jnp.dot(flattened_up.astype(jnp.float32), output_basis.astype(jnp.float32), preferred_element_type=jnp.float32)
        projected_down = jnp.dot(flattened_down.astype(jnp.float32), input_basis.astype(jnp.float32), preferred_element_type=jnp.float32)
        output_factor = blocked_cholesky(gram_out + core_penalty_shift * identity_k)
        input_factor = blocked_cholesky(gram_in + core_penalty_shift * identity_k)
        output_contribution, input_contribution, normal_out, normal_in = adapter_summands(projected_up, projected_down, fitting_weight, output_factor, input_factor, core_penalty_shift, ADAPTER_RANK)
        numer_out = jnp.dot(flattened_up.T.astype(jnp.float32), output_contribution.astype(jnp.float32), preferred_element_type=jnp.float32)
        numer_in = jnp.dot(flattened_down.T.astype(jnp.float32), input_contribution.astype(jnp.float32), preferred_element_type=jnp.float32)
        solve_out = blocked_cholesky(normal_out + basis_penalty_shift * identity_k)
        solve_in = blocked_cholesky(normal_in + basis_penalty_shift * identity_k)
        output_basis = solve_from_right(numer_out, solve_out).astype(jnp.bfloat16)
        input_basis = solve_from_right(numer_in, solve_in).astype(jnp.bfloat16)
    return (output_basis, input_basis)
```

```python
import functools

import jax
import jax.numpy as jnp
from jax import lax
from jax.experimental import pallas as pl
from jax.experimental.pallas import tpu as pltpu
from jax.sharding import PartitionSpec as P

MODEL_WIDTH = 12288
PRECISE = lax.Precision.HIGHEST
CORE_RIDGE = 0.25
BASIS_PENALTY = 0.1
PANEL = 8
LANES = 128
GROUP = 128


def dot(a, b, dims, precision=PRECISE):
    return lax.dot_general(
        a, b, (dims, ((), ())), preferred_element_type=jnp.float32, precision=precision
    )


def spread_row(row):
    return jnp.broadcast_to(row, (PANEL, LANES))


def negated_panel_inverse(columns, sublane):
    columns = list(columns)
    for j in range(0, PANEL, 2):
        at_first, at_second = sublane == j, sublane == j + 1
        first, second = columns[j], columns[j + 1]
        a = spread_row(first[j : j + 1, :])
        b = spread_row(first[j + 1 : j + 2, :])
        d = spread_row(second[j + 1 : j + 2, :])
        scale = 1.0 / (a * d - b * b)
        a, b, d = a * scale, b * scale, d * scale
        for i in range(PANEL):
            if i not in (j, j + 1):
                one = spread_row(columns[i][j : j + 1, :])
                two = spread_row(columns[i][j + 1 : j + 2, :])
                top, low = d * one - b * two, a * two - b * one
                other = columns[i] - first * top - second * low
                columns[i] = jnp.where(at_first, top, jnp.where(at_second, low, other))
        columns[j] = jnp.where(
            at_first, -d, jnp.where(at_second, b, first * d - second * b)
        )
        columns[j + 1] = jnp.where(
            at_first, b, jnp.where(at_second, -a, second * a - first * b)
        )
    return columns


def swept_blocks(blocks):
    sublane = lax.broadcasted_iota(jnp.int32, (PANEL, LANES), 0)
    lane = lax.broadcasted_iota(jnp.int32, (PANEL, LANES), 1)
    panels = LANES // PANEL
    states = [[block[PANEL * t : PANEL * (t + 1), :] for t in range(panels)] for block in blocks]
    for t in range(panels):
        first = PANEL * t
        inside = (lane >= first) & (lane < first + PANEL)
        for rows in states:
            pivot_rows = rows[t]
            columns = [
                jnp.broadcast_to(pivot_rows[:, first + i : first + i + 1], (PANEL, LANES))
                for i in range(PANEL)
            ]
            columns = negated_panel_inverse(columns, sublane)
            terms = [columns[i] * spread_row(pivot_rows[i : i + 1, :]) for i in range(PANEL)]
            while len(terms) > 1:
                terms = [terms[i] + terms[i + 1] for i in range(0, len(terms), 2)]
            swept = -terms[0]
            for i in range(PANEL):
                swept = jnp.where(lane == first + i, columns[i], swept)
            change = dot(pivot_rows, swept, ((0,), (0,)))
            for s in range(panels):
                if s == t:
                    continue
                kept = jnp.where(inside, 0.0, rows[s])
                if s == t + 1:
                    parts = [
                        jnp.broadcast_to(rows[s][:, first + i : first + i + 1], (PANEL, LANES))
                        * spread_row(swept[i : i + 1, :])
                        for i in range(PANEL)
                    ]
                    while len(parts) > 1:
                        parts = [parts[i] + parts[i + 1] for i in range(0, len(parts), 2)]
                    rows[s] = kept - parts[0]
                else:
                    rows[s] = kept - change[PANEL * s : PANEL * (s + 1), :]
            rows[t] = swept
    return [jnp.concatenate(rows, axis=0) for rows in states]


def sweep_all(held_ref):
    count, size, _ = held_ref.shape

    def step(k, carry):
        span = pl.ds(pl.multiple_of(k * LANES, LANES), LANES)
        swept = swept_blocks([held_ref[i, span, span] for i in range(count)])
        for i in range(count):
            rows = held_ref[i, span, :]
            columns = -dot(rows, swept[i], ((0,), (0,)))
            scaled = -dot(swept[i], rows, ((1,), (0,)))
            held_ref[i] = held_ref[i] - dot(columns, rows, ((1,), (0,)))
            held_ref[i, :, span] = columns
            held_ref[i, span, :] = scaled
            held_ref[i, span, span] = swept[i]
        return carry

    lax.fori_loop(0, size // LANES, step, 0)


def add_ridge(matrix, ridge):
    row = lax.broadcasted_iota(jnp.int32, matrix.shape, 0)
    column = lax.broadcasted_iota(jnp.int32, matrix.shape, 1)
    return matrix + jnp.where(row == column, ridge, 0.0)


VMEM = pl.BlockSpec(memory_space=pltpu.VMEM)
SMEM = pl.BlockSpec(memory_space=pltpu.SMEM)
NN = ((1,), (0,))
NT = ((1,), (1,))
TN = ((0,), (0,))


def call(kernel, outs, ins, scratch=(), flops=0, name=None):
    return pl.pallas_call(
        kernel,
        out_shape=outs,
        in_specs=[SMEM] + [VMEM] * (len(ins) - 1),
        out_specs=jax.tree.map(lambda _: VMEM, outs),
        scratch_shapes=list(scratch),
        compiler_params=pltpu.CompilerParams(vmem_limit_bytes=40 * 2**20),
        cost_estimate=pl.CostEstimate(flops=flops, bytes_accessed=4_000_000, transcendentals=0),
        name=name,
    )(*ins)


def sizes_of(shape, dtype):
    return jax.ShapeDtypeStruct(shape, dtype)


def gram_inverse_kernel(ridge, place_ref, s0, s1, s2, s3, inverse_ref, held):
    size = held.shape[1]
    strip = s0.shape[0]
    for k, piece in enumerate((s0, s1, s2, s3)):
        owner = lax.rem(place_ref[2] + 4 - k, 4)
        held[0, pl.ds(pl.multiple_of(owner * strip, strip), strip), :] = piece[...]
    held[0] = add_ridge(held[0], ridge)
    sweep_all(held)
    inverse_ref[...] = -held[0]


def gram_inverse(place, strips):
    width = strips[0].shape[1]
    return call(
        functools.partial(gram_inverse_kernel, CORE_RIDGE * MODEL_WIDTH),
        sizes_of((width, width), jnp.float32),
        (place, *strips),
        [pltpu.VMEM((1, width, width), jnp.float32)],
        25_000_000_000,
        "invert_gram",
    )


def normal_inverse_kernel(place_ref, ridge_ref, s0, s1, s2, s3, inverse_ref, held):
    strip = s0.shape[0]
    piece = strip // 4
    for k, rows in enumerate((s0, s1, s2, s3)):
        owner = lax.rem(place_ref[0] + 4 - k, 4)
        for j in range(4):
            inner = lax.rem(place_ref[2] + 4 - j, 4)
            start = pl.multiple_of(owner * strip + inner * piece, piece)
            held[0, pl.ds(start, piece), :] = rows[piece * j : piece * (j + 1), :]
    held[0] = add_ridge(held[0], ridge_ref[0, 0])
    sweep_all(held)
    inverse_ref[...] = -held[0]


def normal_inverse(place, ridge, strips):
    width = strips[0].shape[1]
    return call(
        normal_inverse_kernel,
        sizes_of((width, width), jnp.float32),
        (place, ridge, *strips),
        [pltpu.VMEM((1, width, width), jnp.float32)],
        25_000_000_000,
        "invert_normal",
    )


def fit_kernel(rank, ridge, place_ref, inverse_ref, weight_ref, p0, p1, p2, p3, fit_ref, small_ref):
    row = lax.broadcasted_iota(jnp.int32, (GROUP, GROUP), 0) // rank
    column = lax.broadcasted_iota(jnp.int32, (GROUP, GROUP), 1) // rank
    same_slot = row == column
    for k, projected in enumerate((p0, p1, p2, p3)):
        owner = lax.rem(place_ref[0] + 4 - k, 4)
        span = pl.ds(pl.multiple_of(owner * GROUP, GROUP), GROUP)
        fit = dot(projected[...], inverse_ref[...], NN)
        fit_ref[span, :] = fit
        weight = jnp.broadcast_to(weight_ref[span, :], (GROUP, GROUP))
        mask = jnp.where(same_slot, weight, 0.0)
        cross = dot(projected[...], fit, NT)
        curve = cross - ridge * dot(fit, fit, NT)
        small_ref[0, span, :] = cross * mask
        small_ref[1, span, :] = curve * mask


def fit_slots(place, inverse, weight, projected, rank):
    rows, width = projected[0].shape
    return call(
        functools.partial(fit_kernel, rank, CORE_RIDGE * MODEL_WIDTH),
        (
            sizes_of((4 * rows, width), jnp.float32),
            sizes_of((2, 4 * rows, GROUP), jnp.float32),
        ),
        (place, inverse, weight, *projected),
        (),
        4_000_000_000,
        "fit_slots",
    )


def load_kernel(place_ref, fit_ref, small_ref, push_ref, normal_ref, load):
    for start in range(0, fit_ref.shape[0], GROUP):
        group = slice(start, start + GROUP)
        fit = fit_ref[group, :]
        push_ref[group, :] = dot(small_ref[0, group, :], fit, NN).astype(jnp.bfloat16)
        load[group, :] = dot(small_ref[1, group, :], fit, NN)
    span = pl.ds(pl.multiple_of(place_ref[0] * LANES, LANES), LANES)
    normal_ref[...] = dot(load[:, span], fit_ref[...], TN)


def load_slots(place, fit, small):
    rows, width = fit.shape
    return call(
        load_kernel,
        (sizes_of((rows, width), jnp.bfloat16), sizes_of((LANES, width), jnp.float32)),
        (place, fit, small),
        [pltpu.VMEM((rows, width), jnp.float32)],
        4_000_000_000,
        "load_slots",
    )


def numer_kernel(
    place_ref, up_ref, down_ref, out_push, in_push, own_ref, forward, backward, later_1, later_3
):
    width = out_push.shape[1]
    part = own_ref.shape[0]
    half = part // 2
    for k in range(4):
        owner = lax.rem(place_ref[2] + k, 4)
        span = pl.ds(pl.multiple_of(owner * part, LANES), part)
        for side, (factor, push) in enumerate(((up_ref, out_push), (down_ref, in_push))):
            term = dot(factor[:, span], push[...], TN, None)
            columns = slice(side * width, (side + 1) * width)
            first, second = term[:half], term[half:]
            if k == 0:
                own_ref[:, columns] = term
            elif k == 1:
                later_1[:, columns] = first
                forward[half:, columns] = second.astype(jnp.bfloat16)
            elif k == 2:
                forward[:half, columns] = first.astype(jnp.bfloat16)
                backward[half:, columns] = second.astype(jnp.bfloat16)
            else:
                backward[:half, columns] = first.astype(jnp.bfloat16)
                later_3[:, columns] = second


def numer_parts(place, up, down, out_push, in_push):
    part = up.shape[1] // 4
    width = 2 * out_push.shape[1]
    outs = (sizes_of((part, width), jnp.float32),)
    outs += (sizes_of((part, width), jnp.bfloat16),) * 2
    outs += (sizes_of((part // 2, width), jnp.float32),) * 2
    return call(
        numer_kernel,
        outs,
        (place, up, down, out_push, in_push),
        (),
        2_000_000_000,
        "numer_parts",
    )


def solve_kernel(place_ref, own_inverse, other_inverse, own_ref, *refs):
    *parts, rows_ref = refs
    total = own_ref[...]
    for part in parts:
        total = total + part[...].astype(jnp.float32)
    width = own_inverse.shape[0]
    core = place_ref[1]

    def write(first, second):
        rows_ref[:, :width] = dot(total[:, :width], first[...], NN).astype(jnp.bfloat16)
        rows_ref[:, width:] = dot(total[:, width:], second[...], NN).astype(jnp.bfloat16)

    @pl.when(core == 0)
    def _():
        write(own_inverse, other_inverse)

    @pl.when(core != 0)
    def _():
        write(other_inverse, own_inverse)


def solve_rows(place, own_inverse, other_inverse, own, parts):
    return call(
        solve_kernel,
        sizes_of(own.shape, jnp.bfloat16),
        (place, own_inverse, other_inverse, own, *parts),
        (),
        400_000_000,
        "solve_rows",
    )


PIECES = (0, 4, 7, 3, 1, 5, 6, 2)


def place_kernel(place_ref, own, last, top, bottom, following, out_ref, in_ref):
    width = out_ref.shape[1]
    part = own.shape[0]
    half = part // 2
    piece = part // 8
    chunks = ((0, 0, own), (1, 0, last), (2, 0, top), (2, half, bottom), (3, 0, following))
    for k, offset, chunk in chunks:
        owner = lax.rem(place_ref[2] + 4 - k, 4)
        for row in range(0, chunk.shape[0], piece):
            inner = lax.rem(place_ref[3] + PIECES[(offset + row) // piece], 8)
            span = pl.ds(pl.multiple_of(owner * part + inner * piece, piece), piece)
            out_ref[span, :] = chunk[row : row + piece, :width]
            in_ref[span, :] = chunk[row : row + piece, width:]


def place_rows(place, chunks):
    part, width = chunks[0].shape
    outs = (sizes_of((4 * part, width // 2), jnp.bfloat16),) * 2
    return call(place_kernel, outs, (place, *chunks), (), 0, "place_rows")


def shifted(value, axis, k):
    count = lax.axis_size(axis)
    return lax.ppermute(value, axis, [(i, (i + k) % count) for i in range(count)])


def partner(value, axis, bit):
    return lax.ppermute(value, axis, [(i, i ^ bit) for i in range(lax.axis_size(axis))])


def sum_over(value, axis):
    bit = 1
    while bit < lax.axis_size(axis):
        value = value + partner(value, axis, bit)
        bit *= 2
    return value


def piece_of(value, axis, k):
    count = lax.axis_size(axis)
    size = value.shape[0] // count
    return lax.dynamic_slice_in_dim(value, ((lax.axis_index(axis) + k) % count) * size, size, 0)


def scatter_over(value, axis):
    total = piece_of(value, axis, 0)
    for k in range(1, lax.axis_size(axis)):
        total = total + shifted(piece_of(value, axis, k), axis, k)
    return total


def gather_over(value, axis):
    return [value] + [shifted(value, axis, k) for k in range(1, lax.axis_size(axis))]


def after(value, other):
    return lax.optimization_barrier((value, other))[0]


def local(
    output_basis,
    input_basis,
    adapter_up_factor,
    adapter_down_factor,
    slot_adapter_index,
    shard_live_counts,
    adapter_usage_weight,
):
    slots, rank, width = adapter_up_factor.shape
    basis_width = output_basis.shape[1]
    x, core, y, z = (lax.axis_index(axis) for axis in ("x", "core", "y", "z"))
    place = jnp.stack([x, core, y, z]).astype(jnp.int32)
    first_core = core == 0

    def split_sides(out_value, in_value):
        mine = jnp.where(first_core, out_value, in_value)
        theirs = jnp.where(first_core, in_value, out_value)
        return mine + partner(theirs, "core", 1)

    strips = []
    for basis in (output_basis, input_basis):
        columns = lax.dynamic_slice_in_dim(basis, y * LANES, LANES, 1)
        strips.append(dot(columns, basis, TN, None))
    strip = sum(gather_over(split_sides(*strips), "x"))

    up = adapter_up_factor.reshape(slots * rank, width)
    down = adapter_down_factor.reshape(slots * rank, width)
    projected = split_sides(
        jnp.dot(up, output_basis, preferred_element_type=jnp.float32),
        jnp.dot(down, input_basis, preferred_element_type=jnp.float32),
    )
    projected = after(projected, strip)
    inverse = gram_inverse(place, gather_over(strip, "y"))
    projected = gather_over(scatter_over(projected, "x"), "x")

    table_index = jnp.arange(adapter_usage_weight.shape[0], dtype=jnp.int32)
    looked = jnp.sum(
        jnp.where(
            slot_adapter_index[:, None] == table_index[None, :], adapter_usage_weight[None, :], 0.0
        ),
        axis=1,
    )
    slot_index = jnp.arange(slots, dtype=jnp.int32)
    weight = jnp.where(slot_index < shard_live_counts[y * lax.axis_size("z") + z], looked, 0.0)
    weight_rows = jnp.broadcast_to(weight[:, None], (slots, rank)).reshape(slots * rank, 1)
    every_adapter = jnp.sum(shard_live_counts).astype(jnp.float32)
    ridge = BASIS_PENALTY * rank * basis_width * every_adapter / MODEL_WIDTH

    fit, small = fit_slots(place, inverse, weight_rows, projected, rank)
    push, normal = load_slots(place, fit, partner(small, "core", 1))

    summed = sum_over(scatter_over(normal, "y"), "z")
    normal = gather_over(jnp.concatenate(gather_over(summed, "y"), axis=0), "x")

    other_push = partner(push, "core", 1)
    out_push = jnp.where(first_core, push, other_push)
    in_push = jnp.where(first_core, other_push, push)
    own, forward, backward, later_1, later_3 = numer_parts(place, up, down, out_push, in_push)
    half = later_1.shape[0]
    wide = jnp.float32
    forward, backward = shifted(forward, "y", 1), shifted(backward, "y", 3)
    forward, backward = after(forward, summed), after(backward, summed)
    from_last = shifted((later_1 + forward[:half].astype(wide)).astype(jnp.bfloat16), "y", 1)
    from_next = shifted((later_3 + backward[half:].astype(wide)).astype(jnp.bfloat16), "y", 3)
    numer = own + jnp.concatenate(
        [
            from_last.astype(wide) + backward[:half].astype(wide),
            forward[half:].astype(wide) + from_next.astype(wide),
        ],
        axis=0,
    )
    sent = numer.astype(jnp.bfloat16)
    *normal, last = normal
    normal.append(after(last, sent))
    own = piece_of(numer, "z", 0)
    parts = [shifted(piece_of(sent, "z", k), "z", k) for k in range(1, lax.axis_size("z"))]

    inverse = normal_inverse(place, ridge.reshape(1, 1), normal)
    other_inverse = partner(lax.optimization_barrier((inverse, *parts))[0], "core", 1)
    rows = solve_rows(place, inverse, other_inverse, own, parts)

    rows = jnp.concatenate([rows, partner(rows, "z", 4)], axis=0)
    rows = jnp.concatenate([rows] + [shifted(rows, "z", k) for k in (1, 7, 2)], axis=0)
    half = rows.shape[0] // 2
    last, following = shifted(rows, "y", 1), shifted(rows, "y", 3)
    top, bottom = shifted(last[:half], "y", 1), shifted(following[half:], "y", 3)
    return place_rows(place, (rows, last, top, bottom, following))


def solution(mesh):
    fine = jax.sharding.Mesh(mesh.devices.reshape(4, 8, 4, 2), ("y", "z", "x", "core"))
    lib, mp = ("y", "z"), ("x", "core")
    placed = (
        P(mp, None),
        P(mp, None),
        P(lib, None, mp),
        P(lib, None, mp),
        P(lib),
        P(),
        P(),
    )
    return jax.shard_map(
        local, mesh=fine, in_specs=placed, out_specs=(P(mp, None), P(mp, None)), check_vma=False
    )
```

```python
import functools

import jax
import jax.numpy as jnp
from jax import lax
from jax.experimental import pallas as pl
from jax.experimental.pallas import tpu as pltpu
from jax.sharding import PartitionSpec as P

MODEL_WIDTH = 12288
PRECISE = lax.Precision.HIGHEST
CORE_RIDGE = 0.25
BASIS_PENALTY = 0.1
PANEL = 8
LANES = 128
GROUP = 128


def dot(a, b, dims, precision=PRECISE):
    return lax.dot_general(
        a, b, (dims, ((), ())), preferred_element_type=jnp.float32, precision=precision
    )


def spread_row(row):
    return jnp.broadcast_to(row, (PANEL, LANES))


def negated_panel_inverse(columns, sublane):
    columns = list(columns)
    for j in range(0, PANEL, 2):
        at_first, at_second = sublane == j, sublane == j + 1
        first, second = columns[j], columns[j + 1]
        a = spread_row(first[j : j + 1, :])
        b = spread_row(first[j + 1 : j + 2, :])
        d = spread_row(second[j + 1 : j + 2, :])
        scale = 1.0 / (a * d - b * b)
        a, b, d = a * scale, b * scale, d * scale
        for i in range(PANEL):
            if i not in (j, j + 1):
                one = spread_row(columns[i][j : j + 1, :])
                two = spread_row(columns[i][j + 1 : j + 2, :])
                top, low = d * one - b * two, a * two - b * one
                other = columns[i] - first * top - second * low
                columns[i] = jnp.where(at_first, top, jnp.where(at_second, low, other))
        columns[j] = jnp.where(
            at_first, -d, jnp.where(at_second, b, first * d - second * b)
        )
        columns[j + 1] = jnp.where(
            at_first, b, jnp.where(at_second, -a, second * a - first * b)
        )
    return columns


def sum_of(terms):
    while len(terms) > 1:
        odd = terms[-1:] if len(terms) % 2 else []
        terms = [terms[i] + terms[i + 1] for i in range(0, len(terms) - 1, 2)] + odd
    return terms[0]


def spread_columns(rows, first):
    return [
        jnp.broadcast_to(rows[:, first + i : first + i + 1], (PANEL, LANES)) for i in range(PANEL)
    ]


def swept_panel(rows, first, lane, sublane):
    columns = negated_panel_inverse(spread_columns(rows, first), sublane)
    swept = -sum_of([columns[i] * spread_row(rows[i : i + 1, :]) for i in range(PANEL)])
    for i in range(PANEL):
        swept = jnp.where(lane == first + i, columns[i], swept)
    return swept


def updated_panel(rows, first, swept, lane):
    columns = spread_columns(rows, first)
    change = sum_of([columns[i] * spread_row(swept[i : i + 1, :]) for i in range(PANEL)])
    return jnp.where((lane >= first) & (lane < first + PANEL), 0.0, rows) - change


def swept_block(block):
    sublane = lax.broadcasted_iota(jnp.int32, (PANEL, LANES), 0)
    lane = lax.broadcasted_iota(jnp.int32, (PANEL, LANES), 1)
    panels = LANES // PANEL
    rows = [block[PANEL * t : PANEL * (t + 1), :] for t in range(panels)]
    for t in range(0, panels, 2):
        start, middle, stop = PANEL * t, PANEL * (t + 1), PANEL * (t + 2)
        first = rows[t]
        first_swept = swept_panel(first, start, lane, sublane)
        second = updated_panel(rows[t + 1], start, first_swept, lane)
        second_swept = swept_panel(second, middle, lane, sublane)
        if stop < LANES:
            ahead = updated_panel(rows[t + 2], start, first_swept, lane)
            ahead = updated_panel(ahead, middle, second_swept, lane)
        masked = jnp.where((lane >= middle) & (lane < stop), 0.0, first_swept)
        change = dot(
            jnp.concatenate([first, second], axis=0),
            jnp.concatenate([masked, second_swept], axis=0),
            ((0,), (0,)),
        )
        inside = (lane >= start) & (lane < stop)
        for s in range(panels):
            if s == t:
                rows[s] = updated_panel(first_swept, middle, second_swept, lane)
            elif s == t + 1:
                rows[s] = second_swept
            elif s == t + 2:
                rows[s] = ahead
            else:
                rows[s] = jnp.where(inside, 0.0, rows[s]) - change[PANEL * s : PANEL * (s + 1), :]
    return jnp.concatenate(rows, axis=0)


def sweep_all(held_ref, first, last):
    def step(k, carry):
        span = pl.ds(pl.multiple_of(k * LANES, LANES), LANES)
        swept = swept_block(held_ref[span, span])
        rows = held_ref[span, :]
        columns = -dot(rows, swept, ((0,), (0,)))
        scaled = -dot(swept, rows, ((1,), (0,)))
        held_ref[...] = held_ref[...] - dot(columns, rows, ((1,), (0,)))
        held_ref[:, span] = columns
        held_ref[span, :] = scaled
        held_ref[span, span] = swept
        return carry

    lax.fori_loop(first, last, step, 0)


def add_ridge(matrix, ridge):
    row = lax.broadcasted_iota(jnp.int32, matrix.shape, 0)
    column = lax.broadcasted_iota(jnp.int32, matrix.shape, 1)
    return matrix + jnp.where(row == column, ridge, 0.0)


VMEM = pl.BlockSpec(memory_space=pltpu.VMEM)
SMEM = pl.BlockSpec(memory_space=pltpu.SMEM)
NN = ((1,), (0,))
NT = ((1,), (1,))
TN = ((0,), (0,))


def call(kernel, outs, ins, scratch=(), flops=0, name=None, limit=12):
    return pl.pallas_call(
        kernel,
        out_shape=outs,
        in_specs=[SMEM] + [VMEM] * (len(ins) - 1),
        out_specs=jax.tree.map(lambda _: VMEM, outs),
        scratch_shapes=list(scratch),
        compiler_params=pltpu.CompilerParams(vmem_limit_bytes=limit * 2**20),
        cost_estimate=pl.CostEstimate(flops=flops, bytes_accessed=4_000_000, transcendentals=0),
        name=name,
    )(*ins)


def sizes_of(shape, dtype):
    return jax.ShapeDtypeStruct(shape, dtype)


def first_half_kernel(ridge, place_ref, s0, s1, s2, s3, held_ref):
    strip = s0.shape[0]
    for k, piece in enumerate((s0, s1, s2, s3)):
        owner = lax.rem(place_ref[2] + 4 - k, 4)
        held_ref[pl.ds(pl.multiple_of(owner * strip, strip), strip), :] = piece[...]
    held_ref[...] = add_ridge(held_ref[...], ridge)
    sweep_all(held_ref, 0, held_ref.shape[0] // LANES // 2)


def first_half(place, strips):
    width = strips[0].shape[1]
    return call(
        functools.partial(first_half_kernel, CORE_RIDGE * MODEL_WIDTH),
        sizes_of((width, width), jnp.float32),
        (place, *strips),
        (),
        12_000_000_000,
        "invert_gram_first",
    )


def second_half_kernel(place_ref, begun_ref, held_ref):
    held_ref[...] = begun_ref[...]
    blocks = held_ref.shape[0] // LANES
    sweep_all(held_ref, blocks // 2, blocks)


def second_half(place, begun):
    return call(
        second_half_kernel,
        sizes_of(begun.shape, jnp.float32),
        (place, begun),
        (),
        12_000_000_000,
        "invert_gram_second",
    )


def normal_inverse_kernel(place_ref, ridge_ref, strips_ref, held_ref):
    piece = strips_ref.shape[0] // 16
    for k in range(16):
        inner = lax.rem(place_ref[2] + 4 - k % 4, 4)
        start = pl.multiple_of(k // 4 * 4 * piece + inner * piece, piece)
        held_ref[pl.ds(start, piece), :] = strips_ref[piece * k : piece * (k + 1), :]
    held_ref[...] = add_ridge(held_ref[...], ridge_ref[0, 0])
    sweep_all(held_ref, 0, held_ref.shape[0] // LANES)


def normal_inverse(place, ridge, strips):
    return call(
        normal_inverse_kernel,
        sizes_of(strips.shape, jnp.float32),
        (place, ridge, strips),
        (),
        25_000_000_000,
        "invert_normal",
    )


def fit_kernel(rank, ridge, place_ref, negated_ref, weight_ref, p0, p1, p2, p3, fit_ref, small_ref):
    row = lax.broadcasted_iota(jnp.int32, (GROUP, GROUP), 0) // rank
    column = lax.broadcasted_iota(jnp.int32, (GROUP, GROUP), 1) // rank
    same_slot = row == column
    for k, projected in enumerate((p0, p1, p2, p3)):
        owner = lax.rem(place_ref[0] + 4 - k, 4)
        span = pl.ds(pl.multiple_of(owner * GROUP, GROUP), GROUP)
        fit = -dot(projected[...], negated_ref[...], NN)
        fit_ref[span, :] = fit
        weight = jnp.broadcast_to(weight_ref[span, :], (GROUP, GROUP))
        mask = jnp.where(same_slot, weight, 0.0)
        cross = dot(projected[...], fit, NT)
        curve = cross - ridge * dot(fit, fit, NT)
        small_ref[0, span, :] = cross * mask
        small_ref[1, span, :] = curve * mask


def fit_slots(place, inverse, weight, projected, rank):
    rows, width = projected[0].shape
    return call(
        functools.partial(fit_kernel, rank, CORE_RIDGE * MODEL_WIDTH),
        (
            sizes_of((4 * rows, width), jnp.float32),
            sizes_of((2, 4 * rows, GROUP), jnp.float32),
        ),
        (place, inverse, weight, *projected),
        (),
        4_000_000_000,
        "fit_slots",
    )


def load_kernel(place_ref, fit_ref, small_ref, push_ref, normal_ref, load):
    for start in range(0, fit_ref.shape[0], GROUP):
        group = slice(start, start + GROUP)
        fit = fit_ref[group, :]
        push_ref[group, :] = dot(small_ref[0, group, :], fit, NN).astype(jnp.bfloat16)
        load[group, :] = dot(small_ref[1, group, :], fit, NN)
    span = pl.ds(pl.multiple_of(place_ref[0] * LANES, LANES), LANES)
    normal_ref[...] = dot(load[:, span], fit_ref[...], TN)


def load_slots(place, fit, small):
    rows, width = fit.shape
    return call(
        load_kernel,
        (sizes_of((rows, width), jnp.bfloat16), sizes_of((LANES, width), jnp.float32)),
        (place, fit, small),
        [pltpu.VMEM((rows, width), jnp.float32)],
        4_000_000_000,
        "load_slots",
    )


def numer_kernel(
    place_ref, up_ref, down_ref, out_push, in_push, own_ref, forward, backward, later_1, later_3
):
    width = out_push.shape[1]
    part = own_ref.shape[0]
    half = part // 2
    for k in range(4):
        owner = lax.rem(place_ref[2] + k, 4)
        span = pl.ds(pl.multiple_of(owner * part, LANES), part)
        for side, (factor, push) in enumerate(((up_ref, out_push), (down_ref, in_push))):
            term = dot(factor[:, span], push[...], TN, None)
            columns = slice(side * width, (side + 1) * width)
            first, second = term[:half], term[half:]
            if k == 0:
                own_ref[:, columns] = term
            elif k == 1:
                later_1[:, columns] = first
                forward[half:, columns] = second.astype(jnp.bfloat16)
            elif k == 2:
                forward[:half, columns] = first.astype(jnp.bfloat16)
                backward[half:, columns] = second.astype(jnp.bfloat16)
            else:
                backward[:half, columns] = first.astype(jnp.bfloat16)
                later_3[:, columns] = second


def numer_parts(place, up, down, out_push, in_push):
    part = up.shape[1] // 4
    width = 2 * out_push.shape[1]
    outs = (sizes_of((part, width), jnp.float32),)
    outs += (sizes_of((part, width), jnp.bfloat16),) * 2
    outs += (sizes_of((part // 2, width), jnp.float32),) * 2
    return call(
        numer_kernel,
        outs,
        (place, up, down, out_push, in_push),
        (),
        2_000_000_000,
        "numer_parts",
        24,
    )


def solve_kernel(place_ref, own_inverse, other_inverse, own_ref, *refs):
    *parts, rows_ref = refs
    total = own_ref[...]
    for part in parts:
        total = total + part[...].astype(jnp.float32)
    width = own_inverse.shape[0]
    core = place_ref[1]

    def write(first, second):
        rows_ref[:, :width] = (-dot(total[:, :width], first[...], NN)).astype(jnp.bfloat16)
        rows_ref[:, width:] = (-dot(total[:, width:], second[...], NN)).astype(jnp.bfloat16)

    @pl.when(core == 0)
    def _():
        write(own_inverse, other_inverse)

    @pl.when(core != 0)
    def _():
        write(other_inverse, own_inverse)


def solve_rows(place, own_inverse, other_inverse, own, parts):
    return call(
        solve_kernel,
        sizes_of(own.shape, jnp.bfloat16),
        (place, own_inverse, other_inverse, own, *parts),
        (),
        400_000_000,
        "solve_rows",
    )


PIECES = (0, 4, 7, 3, 1, 5, 6, 2)


def place_kernel(place_ref, own, last, top, bottom, following, out_ref, in_ref):
    width = out_ref.shape[1]
    part = own.shape[0]
    half = part // 2
    piece = part // 8
    chunks = ((0, 0, own), (1, 0, last), (2, 0, top), (2, half, bottom), (3, 0, following))
    for k, offset, chunk in chunks:
        owner = lax.rem(place_ref[2] + 4 - k, 4)
        for row in range(0, chunk.shape[0], piece):
            inner = lax.rem(place_ref[3] + PIECES[(offset + row) // piece], 8)
            span = pl.ds(pl.multiple_of(owner * part + inner * piece, piece), piece)
            out_ref[span, :] = chunk[row : row + piece, :width]
            in_ref[span, :] = chunk[row : row + piece, width:]


def place_rows(place, chunks):
    part, width = chunks[0].shape
    outs = (sizes_of((4 * part, width // 2), jnp.bfloat16),) * 2
    return call(place_kernel, outs, (place, *chunks), (), 0, "place_rows", 16)


def shifted(value, axis, k):
    count = lax.axis_size(axis)
    return lax.ppermute(value, axis, [(i, (i + k) % count) for i in range(count)])


def partner(value, axis, bit):
    return lax.ppermute(value, axis, [(i, i ^ bit) for i in range(lax.axis_size(axis))])


def sum_over(value, axis):
    bit = 1
    while bit < lax.axis_size(axis):
        value = value + partner(value, axis, bit)
        bit *= 2
    return value


def piece_of(value, axis, k):
    count = lax.axis_size(axis)
    size = value.shape[0] // count
    return lax.dynamic_slice_in_dim(value, ((lax.axis_index(axis) + k) % count) * size, size, 0)


def scatter_over(value, axis):
    total = piece_of(value, axis, 0)
    for k in range(1, lax.axis_size(axis)):
        total = total + shifted(piece_of(value, axis, k), axis, k)
    return total


def gather_over(value, axis):
    return [value] + [shifted(value, axis, k) for k in range(1, lax.axis_size(axis))]


def after(value, other):
    return lax.optimization_barrier((value, other))[0]


def local(
    output_basis,
    input_basis,
    adapter_up_factor,
    adapter_down_factor,
    slot_adapter_index,
    shard_live_counts,
    adapter_usage_weight,
):
    slots, rank, width = adapter_up_factor.shape
    basis_width = output_basis.shape[1]
    x, core, y, z = (lax.axis_index(axis) for axis in ("x", "core", "y", "z"))
    place = jnp.stack([x, core, y, z]).astype(jnp.int32)
    first_core = core == 0

    def mine_and_theirs(out_value, in_value):
        return jnp.where(first_core, out_value, in_value), jnp.where(first_core, in_value, out_value)

    strips = []
    for basis in (output_basis, input_basis):
        columns = lax.dynamic_slice_in_dim(basis, y * LANES, LANES, 1)
        strips.append(dot(columns, basis, TN, None))
    mine, theirs = mine_and_theirs(*strips)
    strip = sum(gather_over(mine + partner(theirs, "core", 1), "x"))

    up = adapter_up_factor.reshape(slots * rank, width)
    down = adapter_down_factor.reshape(slots * rank, width)
    mine, theirs = mine_and_theirs(
        jnp.dot(after(up, theirs), output_basis, preferred_element_type=jnp.float32),
        jnp.dot(after(down, theirs), input_basis, preferred_element_type=jnp.float32),
    )
    projected = mine + partner(theirs, "core", 1)
    strips = gather_over(strip, "y")
    projected = scatter_over(after(projected, strips[1]), "x")
    begun = first_half(place, strips)
    projected = gather_over(after(projected, begun), "x")
    negated = second_half(place, begun)

    table_index = jnp.arange(adapter_usage_weight.shape[0], dtype=jnp.int32)
    looked = jnp.sum(
        jnp.where(
            slot_adapter_index[:, None] == table_index[None, :], adapter_usage_weight[None, :], 0.0
        ),
        axis=1,
    )
    slot_index = jnp.arange(slots, dtype=jnp.int32)
    weight = jnp.where(slot_index < shard_live_counts[y * lax.axis_size("z") + z], looked, 0.0)
    weight_rows = jnp.broadcast_to(weight[:, None], (slots, rank)).reshape(slots * rank, 1)
    every_adapter = jnp.sum(shard_live_counts).astype(jnp.float32)
    ridge = BASIS_PENALTY * rank * basis_width * every_adapter / MODEL_WIDTH

    fit, small = fit_slots(place, negated, weight_rows, projected, rank)
    push, normal = load_slots(place, fit, partner(small, "core", 1))

    normal = scatter_over(normal, "y")
    push = after(push, normal)
    summed = sum_over(normal, "z")
    normal = jnp.concatenate(gather_over(summed, "y"), axis=0)
    normal = lax.all_gather(normal, "x", axis=0, tiled=True)

    other_push = partner(push, "core", 1)
    out_push = jnp.where(first_core, push, other_push)
    in_push = jnp.where(first_core, other_push, push)
    own, forward, backward, later_1, later_3 = numer_parts(place, up, down, out_push, in_push)
    half = later_1.shape[0]
    wide = jnp.float32
    forward, backward = shifted(forward, "y", 1), shifted(backward, "y", 3)
    forward, backward = after(forward, summed), after(backward, summed)
    low = (later_1 + forward[:half].astype(wide)).astype(jnp.bfloat16)
    high = (later_3 + backward[half:].astype(wide)).astype(jnp.bfloat16)
    from_last, from_next = shifted(low, "y", 1), shifted(high, "y", 3)
    forward, backward = after(forward, low), after(backward, high)
    numer = own + jnp.concatenate(
        [
            from_last.astype(wide) + backward[:half].astype(wide),
            forward[half:].astype(wide) + from_next.astype(wide),
        ],
        axis=0,
    )
    sent = numer.astype(jnp.bfloat16)
    normal = after(normal, sent)
    own = piece_of(numer, "z", 0)
    parts = [shifted(piece_of(sent, "z", k), "z", k) for k in range(1, lax.axis_size("z"))]

    inverse = normal_inverse(place, ridge.reshape(1, 1), normal)
    other_inverse = partner(lax.optimization_barrier((inverse, *parts))[0], "core", 1)
    rows = solve_rows(place, inverse, other_inverse, own, parts)

    rows = jnp.concatenate([rows, partner(rows, "z", 4)], axis=0)
    rows = jnp.concatenate([rows] + [shifted(rows, "z", k) for k in (1, 7, 2)], axis=0)
    half = rows.shape[0] // 2
    last, following = shifted(rows, "y", 1), shifted(rows, "y", 3)
    top, bottom = shifted(last[:half], "y", 1), shifted(following[half:], "y", 3)
    return place_rows(place, (rows, last, top, bottom, following))


def solution(mesh):
    fine = jax.sharding.Mesh(mesh.devices.reshape(4, 8, 4, 2), ("y", "z", "x", "core"))
    lib, mp = ("y", "z"), ("x", "core")
    placed = (
        P(mp, None),
        P(mp, None),
        P(lib, None, mp),
        P(lib, None, mp),
        P(lib),
        P(),
        P(),
    )
    return jax.shard_map(
        local, mesh=fine, in_specs=placed, out_specs=(P(mp, None), P(mp, None)), check_vma=False
    )
```
